32 devices in a mesh: tm: 8 (over y, x, core), space: 4 (over z).
Axes of the slice: x: 2, y: 2, z: 4, core: 2. Of those that a mesh axis runs over, the one named last changes fastest.
Arguments:
- eigvec: bfloat16 [8, 2, 3, 4096, 384], P('tm', None, None, 'space'), may hold values from -1.5 to 1.5
- momenta: int32 [2, 3], replicated, may hold values from -2 to 2
- peram: bfloat16 [8, 2, 384, 4, 384], P('tm', None, 'space'), may hold values from -0.0078125 to 0.0078125
Outputs:
- dressed: bfloat16 [8, 384, 4, 2, 384], P('tm', 'space')
The draws below stay inside these ranges and needn't reach their ends.
All inputs are finite; a program needn't handle non-finite values.
Results may differ from the reference program's by a relative error of at most 0.0073.
Values may be sent and summed in bfloat16 or wider, within the bound.
A program may use at most 128 MiB of HBM per device.

```python
import math
import jax
import jax.numpy as jnp
from jax import lax

NVEC = 384
SPIN = 4
COLORS = 3
LAT = 32
NMOM = 2
VOL = 4096
NT = 8


def place_ends(entries, stream_key, low, high):
    longest = entries.shape.index(max(entries.shape))
    spots = []
    for shift in (0, 1):
        where = [jax.random.randint(jax.random.fold_in(stream_key, axis), (), 0, length) for axis, length in enumerate(entries.shape)]
        where[longest] = (where[longest] + shift) % entries.shape[longest]
        spots.append(tuple(where))
    return entries.at[spots[0]].set(low).at[spots[1]].set(high)


def block_scale(stream_key, shape, split, smallest, high):
    def one(dim, blocks):
        draws = jax.random.uniform(jax.random.fold_in(jax.random.fold_in(stream_key, 6), dim), (blocks,), jnp.float32, smallest / len(split), high / len(split))
        return jnp.repeat(jnp.exp(draws), shape[dim] // blocks).reshape((-1,) + (1,) * (len(shape) - dim - 1))

    gain = one(*split[0])
    for cut in split[1:]:
        gain = gain * one(*cut)
    return gain


def gaussian(key, shape, width, bound, shards=(), kind=jnp.bfloat16):
    loudness = block_scale(key, shape, shards, -0.22, 0.18) if shards else 1.0
    drawn = jax.random.normal(key, shape, jnp.float32) * width * loudness
    return jnp.minimum(jnp.maximum(drawn, -bound), bound).astype(kind)


def setup_inputs(seed: int = 0) -> dict:
    key_list = jax.random.split(jax.random.key(seed), 4)
    return {
        "eigvec": gaussian(key_list[0], (NT, 2, COLORS, VOL, NVEC), ((3 * VOL) ** -0.25), 1.5, ((0, 8), (3, 4))),
        "momenta": place_ends(jax.random.randint(key_list[1], (NMOM, 3), -2, 3), jax.random.fold_in(key_list[1], 1), -2, 2).astype(jnp.int32),
        "peram": gaussian(key_list[2], (NT, 2, NVEC, SPIN, NVEC), (0.2 * NVEC ** -1), 0.0078125, ((0, 8), (2, 4))),
    }


def phase_gram(vectors, momentum):
    sites = jnp.arange(VOL, dtype=jnp.int32)
    coord_x = sites % LAT
    coord_y = (sites // LAT) % LAT
    coord_z = sites // (LAT * LAT)
    winding = jnp.mod(momentum[0] * coord_x + momentum[1] * coord_y + momentum[2] * coord_z, LAT)
    theta = winding.astype(jnp.float32) * (2.0 * math.pi / LAT)
    cosine = jnp.cos(theta)[None, :, None]
    sine = jnp.sin(theta)[None, :, None]
    real_part = vectors[0].astype(jnp.float32)
    imag_part = vectors[1].astype(jnp.float32)
    phased_re = (cosine * real_part + sine * imag_part).astype(jnp.bfloat16)
    phased_im = (cosine * imag_part - sine * real_part).astype(jnp.bfloat16)
    upper = jnp.concatenate([phased_re, phased_im], axis=-1)
    lower = jnp.concatenate([phased_im, -phased_re], axis=-1)
    right = jnp.stack([upper, lower]).reshape(2 * COLORS * VOL, 2 * NVEC)
    left = vectors.reshape(2 * COLORS * VOL, NVEC)
    gram = lax.dot_general(left, right, (((0,), (0,)), ((), ())), preferred_element_type=jnp.float32)
    return gram.astype(jnp.bfloat16)


def apply_pair(operands):
    sink, source, tau = operands
    sink_re = sink[:, :NVEC]
    sink_im = sink[:, NVEC:]
    left = jnp.stack([jnp.concatenate([sink_re, -sink_im], axis=1), jnp.concatenate([sink_im, sink_re], axis=1)], axis=1)
    left = left.reshape(2 * NVEC, 2 * NVEC)
    mixed = jnp.dot(left, tau.reshape(2 * NVEC, SPIN * NVEC), preferred_element_type=jnp.float32)
    mixed = mixed.astype(jnp.bfloat16).reshape(NVEC, 2, SPIN * NVEC)
    mixed_re = mixed[:, 0].reshape(NVEC * SPIN, NVEC)
    mixed_im = mixed[:, 1].reshape(NVEC * SPIN, NVEC)
    source_re = source[:, :NVEC]
    source_im = source[:, NVEC:]
    right = jnp.concatenate([source, jnp.concatenate([-source_im, source_re], axis=1)], axis=0)
    dressed = jnp.dot(jnp.concatenate([mixed_re, mixed_im], axis=1), right, preferred_element_type=jnp.float32)
    return dressed.reshape(NVEC, SPIN, 2, NVEC).astype(jnp.bfloat16)


def reference(eigvec, momenta, peram):
    def both(vectors):
        return jnp.stack([phase_gram(vectors, momenta[0]), phase_gram(vectors, momenta[1])])

    elemental = lax.map(both, eigvec)
    source = elemental[::-1, 1]
    return lax.map(apply_pair, (elemental[:, 0], source, peram))
```

```python
import functools
import math

import jax
import jax.numpy as jnp
from jax import lax
from jax.experimental import pallas as pl
from jax.experimental.pallas import tpu as pltpu
from jax.sharding import PartitionSpec as P

SPIN = 4
COLORS = 3
LAT = 32


def phase_tables(momenta_ref, k, first_site, count):
    sites = first_site + lax.broadcasted_iota(jnp.int32, (count, 128), 0)
    x = sites & (LAT - 1)
    y = (sites >> 5) & (LAT - 1)
    z = sites >> 10
    winding = (momenta_ref[k, 0] * x + momenta_ref[k, 1] * y + momenta_ref[k, 2] * z) & (LAT - 1)
    quadrant = (winding + 4) >> 3
    rest = (winding - (quadrant << 3)).astype(jnp.float32) * (2.0 * math.pi / LAT)
    sq = rest * rest
    sin_r = rest * (
        1.0 + sq * (-1.0 / 6 + sq * (1.0 / 120 + sq * (-1.0 / 5040 + sq * (1.0 / 362880))))
    )
    cos_r = 1.0 + sq * (
        -0.5 + sq * (1.0 / 24 + sq * (-1.0 / 720 + sq * (1.0 / 40320 + sq * (-1.0 / 3628800))))
    )
    odd = (quadrant & 1) == 1
    cos_q = jnp.where(odd, sin_r, cos_r)
    sin_q = jnp.where(odd, cos_r, sin_r)
    cos_t = jnp.where(((quadrant + 1) & 2) == 2, -cos_q, cos_q)
    sin_t = jnp.where((quadrant & 2) == 2, -sin_q, sin_q)
    return cos_t, sin_t


def gram_kernel(k, momenta_ref, vec_ref, out_ref, cos_ref, sin_ref, right_ref, acc_ref):
    step = pl.program_id(0)
    sites = vec_ref.shape[2]
    nvec = vec_ref.shape[3]

    @pl.when(step == 0)
    def _():
        first = lax.axis_index("space") * sites
        cos_t, sin_t = phase_tables(momenta_ref, k, first, sites)
        cos_ref[...] = cos_t
        sin_ref[...] = sin_t

    cosine = cos_ref[...]
    sine = sin_ref[...]
    for lane in range(0, nvec, 128):
        real = vec_ref[0, 0, :, lane : lane + 128].astype(jnp.float32)
        imag = vec_ref[1, 0, :, lane : lane + 128].astype(jnp.float32)
        ph_re = (cosine * real + sine * imag).astype(jnp.bfloat16)
        ph_im = (cosine * imag - sine * real).astype(jnp.bfloat16)
        right_ref[:sites, lane : lane + 128] = ph_re
        right_ref[:sites, nvec + lane : nvec + lane + 128] = ph_im
        right_ref[sites:, lane : lane + 128] = ph_im
        right_ref[sites:, nvec + lane : nvec + lane + 128] = -ph_re
    left = vec_ref[...].reshape(2 * sites, nvec)
    part = lax.dot_general(
        left, right_ref[...], (((0,), (0,)), ((), ())), preferred_element_type=jnp.float32
    )

    @pl.when(step == 0)
    def _():
        acc_ref[...] = part

    @pl.when(step > 0)
    def _():
        acc_ref[...] += part

    @pl.when(step == COLORS - 1)
    def _():
        out_ref[...] = acc_ref[...].astype(out_ref.dtype)


def gram(vectors, momenta, k, dtype):
    sites = vectors.shape[2]
    nvec = vectors.shape[3]
    return pl.pallas_call(
        functools.partial(gram_kernel, k),
        grid=(COLORS,),
        out_shape=jax.ShapeDtypeStruct((nvec, 2 * nvec), dtype),
        in_specs=[
            pl.BlockSpec(memory_space=pltpu.SMEM),
            pl.BlockSpec((2, 1, sites, nvec), lambda c: (0, c, 0, 0)),
        ],
        out_specs=pl.BlockSpec((nvec, 2 * nvec), lambda c: (0, 0)),
        scratch_shapes=[
            pltpu.VMEM((sites, 128), jnp.float32),
            pltpu.VMEM((sites, 128), jnp.float32),
            pltpu.VMEM((2 * sites, 2 * nvec), jnp.bfloat16),
            pltpu.VMEM((nvec, 2 * nvec), jnp.float32),
        ],
        compiler_params=pltpu.CompilerParams(vmem_limit_bytes=40 * 1024 * 1024),
        cost_estimate=pl.CostEstimate(
            flops=8 * COLORS * sites * nvec * nvec,
            bytes_accessed=4 * COLORS * sites * nvec,
            transcendentals=0,
        ),
    )(momenta, vectors)


def complex_left(block_re, block_im):
    rows = block_re.shape[0]
    cols = block_re.shape[1]
    stacked = jnp.stack(
        [
            jnp.concatenate([block_re, -block_im], axis=1),
            jnp.concatenate([block_im, block_re], axis=1),
        ],
        axis=1,
    )
    return stacked.reshape(2 * rows, 2 * cols)


def local(eigvec, momenta, peram):
    vectors = eigvec[0]
    nvec = vectors.shape[3]
    nrows = peram.shape[2]
    tau = peram[0].reshape(2, nrows, SPIN * nvec)
    source_part = gram(vectors, momenta, 1, jnp.float32)
    share = lax.psum_scatter(source_part, "space", scatter_dimension=0, tiled=True).astype(
        jnp.bfloat16
    )
    sink_part = gram(vectors, momenta, 0, jnp.float32)
    times = lax.axis_size("tm")
    share = lax.ppermute(share, "tm", [(i, times - 1 - i) for i in range(times)])
    source = lax.all_gather(share, "space", axis=0, tiled=True)
    block = lax.psum_scatter(sink_part, "space", scatter_dimension=0, tiled=True).astype(
        jnp.bfloat16
    )
    piece = lax.all_gather(tau, "space", axis=1, tiled=True)
    count = piece.shape[1]
    flat = piece.reshape(2 * count, SPIN * nvec)
    mixed = jnp.dot(
        complex_left(block[:, :nvec], block[:, nvec:]), flat, preferred_element_type=jnp.float32
    ).reshape(nrows, 2, SPIN * nvec)
    mixed = mixed.astype(jnp.bfloat16)
    mixed_re = mixed[:, 0].reshape(nrows * SPIN, nvec)
    mixed_im = mixed[:, 1].reshape(nrows * SPIN, nvec)
    source_re = source[:, :nvec]
    source_im = source[:, nvec:]
    right = jnp.concatenate([source, jnp.concatenate([-source_im, source_re], axis=1)], axis=0)
    dressed = jnp.dot(
        jnp.concatenate([mixed_re, mixed_im], axis=1), right, preferred_element_type=jnp.float32
    )
    return dressed.reshape(1, nrows, SPIN, 2, nvec).astype(jnp.bfloat16)


def solution(mesh):
    return jax.shard_map(
        local,
        mesh=mesh,
        in_specs=(P("tm", None, None, "space", None), P(), P("tm", None, "space", None, None)),
        out_specs=P("tm", "space", None, None, None),
        check_vma=False,
    )
```

```python
import functools
import math

import jax
import jax.numpy as jnp
from jax import lax
from jax.experimental import pallas as pl
from jax.experimental.pallas import tpu as pltpu
from jax.sharding import PartitionSpec as P

SPIN = 4
COLORS = 3
LAT = 32
MESH = pl.DeviceIdType.MESH


def phase_tables(momenta_ref, k, first_site, count):
    sites = first_site + lax.broadcasted_iota(jnp.int32, (count, 128), 0)
    x = sites & (LAT - 1)
    y = (sites >> 5) & (LAT - 1)
    z = sites >> 10
    winding = (momenta_ref[k, 0] * x + momenta_ref[k, 1] * y + momenta_ref[k, 2] * z) & (LAT - 1)
    quadrant = (winding + 4) >> 3
    rest = (winding - (quadrant << 3)).astype(jnp.float32) * (2.0 * math.pi / LAT)
    sq = rest * rest
    sin_r = rest * (
        1.0 + sq * (-1.0 / 6 + sq * (1.0 / 120 + sq * (-1.0 / 5040 + sq * (1.0 / 362880))))
    )
    cos_r = 1.0 + sq * (
        -0.5 + sq * (1.0 / 24 + sq * (-1.0 / 720 + sq * (1.0 / 40320 + sq * (-1.0 / 3628800))))
    )
    odd = (quadrant & 1) == 1
    cos_q = jnp.where(odd, sin_r, cos_r)
    sin_q = jnp.where(odd, cos_r, sin_r)
    cos_t = jnp.where(((quadrant + 1) & 2) == 2, -cos_q, cos_q)
    sin_t = jnp.where((quadrant & 2) == 2, -sin_q, sin_q)
    return cos_t, sin_t


def fused_kernel(
    n,
    times,
    momenta_ref,
    vec_hbm,
    tau_ref,
    piece_ref,
    source_ref,
    block_ref,
    vec_ref,
    cos_ref,
    sin_ref,
    right_ref,
    acc_ref,
    part_ref,
    slots_ref,
    share_ref,
    load_sem,
    own_sem,
    hop_send,
    hop_recv,
    sum_send,
    sum_recv,
    all_send,
    all_recv,
):
    me_t = lax.axis_index("tm")
    me = lax.axis_index("space")
    other_t = times - 1 - me_t
    sites = vec_ref.shape[2]
    nvec = vec_ref.shape[3]
    nrows = share_ref.shape[0]

    def load(c):
        return pltpu.make_async_copy(vec_hbm.at[:, c], vec_ref.at[c], load_sem.at[c])

    for c in range(COLORS):
        load(c).start()
    own = pltpu.make_async_copy(tau_ref, piece_ref.at[me], own_sem)
    own.start()

    barrier = pltpu.get_barrier_semaphore()
    for d in range(n):
        peer = lax.rem(me + d, n)
        if d > 0:
            pl.semaphore_signal(barrier, 1, device_id=(me_t, peer), device_id_type=MESH)
        pl.semaphore_signal(barrier, 1, device_id=(other_t, peer), device_id_type=MESH)
    pl.semaphore_wait(barrier, 2 * n - 1)

    def hop(side, h, block, target):
        return pltpu.make_async_remote_copy(
            src_ref=tau_ref if h == 0 else piece_ref.at[block],
            dst_ref=piece_ref.at[block],
            send_sem=hop_send.at[side, h],
            recv_sem=hop_recv.at[side, h],
            device_id=(me_t, target),
            device_id_type=MESH,
        )

    def hop_out(side, h):
        if side == 0:
            return (me >= h) & (me + 1 < n), me - h, me + 1
        return (me + h < n) & (me >= 1), me + h, me - 1

    def hop_in(side, h):
        if side == 0:
            return me >= h + 1, me - 1 - h, me - 1
        return me + 1 + h < n, me + 1 + h, me + 1

    def start_hop(h):
        for side in range(2):
            active, block, target = hop_out(side, h)

            @pl.when(active)
            def _():
                hop(side, h, block, target).start()

    def finish_hop(h):
        for side in range(2):
            active, block, target = hop_in(side, h)

            @pl.when(active)
            def _():
                hop(side, h, block, target).wait_recv()

    def drain_hop(h):
        for side in range(2):
            active, block, target = hop_out(side, h)

            @pl.when(active)
            def _():
                hop(side, h, block, target).wait_send()

    start_hop(0)

    def tables(k):
        cos_t, sin_t = phase_tables(momenta_ref, k, me * sites, sites)
        cos_ref[...] = cos_t
        sin_ref[...] = sin_t

    def add_color(c):
        for lane in range(0, nvec, 128):
            real = vec_ref[c, 0, :, lane : lane + 128].astype(jnp.float32)
            imag = vec_ref[c, 1, :, lane : lane + 128].astype(jnp.float32)
            ph_re = (cos_ref[...] * real + sin_ref[...] * imag).astype(jnp.bfloat16)
            ph_im = (cos_ref[...] * imag - sin_ref[...] * real).astype(jnp.bfloat16)
            right_ref[:sites, lane : lane + 128] = ph_re
            right_ref[:sites, nvec + lane : nvec + lane + 128] = ph_im
            right_ref[sites:, lane : lane + 128] = ph_im
            right_ref[sites:, nvec + lane : nvec + lane + 128] = -ph_re
        acc_ref[...] += lax.dot_general(
            vec_ref[c].reshape(2 * sites, nvec),
            right_ref[...],
            (((0,), (0,)), ((), ())),
            preferred_element_type=jnp.float32,
        )

    def sum_copy(k, d):
        peer = lax.rem(me + d, n)
        return pltpu.make_async_remote_copy(
            src_ref=part_ref.at[k, peer],
            dst_ref=slots_ref.at[k, d - 1],
            send_sem=sum_send.at[k, d - 1],
            recv_sem=sum_recv.at[k, d - 1],
            device_id=(me_t, peer),
            device_id_type=MESH,
        )

    def send_parts(k):
        for j in range(n):
            part_ref[k, j] = acc_ref[j * nrows : (j + 1) * nrows, :].astype(jnp.bfloat16)
        for d in range(1, n):
            sum_copy(k, d).start()

    def summed(k):
        total = part_ref[k, me].astype(jnp.float32)
        for d in range(1, n):
            sum_copy(k, d).wait_recv()
            total = total + slots_ref[k, d - 1].astype(jnp.float32)
        return total.astype(jnp.bfloat16)

    tables(1)
    acc_ref[...] = jnp.zeros_like(acc_ref)

    def source_color(c, carry):
        load(c).wait()
        add_color(c)
        return carry

    lax.fori_loop(0, COLORS, source_color, 0)
    send_parts(1)

    tables(0)
    acc_ref[...] = jnp.zeros_like(acc_ref)

    def sink_color(c, carry):
        add_color(c)
        return carry

    lax.fori_loop(0, COLORS, sink_color, 0)
    send_parts(0)

    share_ref[...] = summed(1)

    def spread(d):
        peer = lax.rem(me + d, n)
        return pltpu.make_async_remote_copy(
            src_ref=share_ref,
            dst_ref=source_ref.at[me],
            send_sem=all_send.at[d],
            recv_sem=all_recv.at[me],
            device_id=(other_t, peer),
            device_id_type=MESH,
        )

    def arrival(j):
        return pltpu.make_async_remote_copy(
            src_ref=share_ref,
            dst_ref=source_ref.at[j],
            send_sem=all_send.at[j],
            recv_sem=all_recv.at[j],
            device_id=(other_t, j),
            device_id_type=MESH,
        )

    for d in range(n):
        spread(d).start()
    for h in range(n - 1):
        finish_hop(h)
        if h + 1 < n - 1:
            start_hop(h + 1)
        if h == 0:
            block_ref[...] = summed(0)
    own.wait()
    for j in range(n):
        arrival(j).wait_recv()
    for d in range(n):
        spread(d).wait_send()
        if d > 0:
            sum_copy(1, d).wait_send()
            sum_copy(0, d).wait_send()
    for h in range(n - 1):
        drain_hop(h)


def fused(vectors, momenta, tau):
    n = lax.axis_size("space")
    times = lax.axis_size("tm")
    sites = vectors.shape[2]
    nvec = vectors.shape[3]
    nrows = tau.shape[1]
    width = tau.shape[2]
    kind = jnp.bfloat16
    return pl.pallas_call(
        functools.partial(fused_kernel, n, times),
        out_shape=(
            jax.ShapeDtypeStruct((n, 2, nrows, width), kind),
            jax.ShapeDtypeStruct((n, nrows, 2 * nvec), kind),
            jax.ShapeDtypeStruct((nrows, 2 * nvec), kind),
        ),
        in_specs=[
            pl.BlockSpec(memory_space=pltpu.SMEM),
            pl.BlockSpec(memory_space=pl.ANY),
            pl.BlockSpec(memory_space=pl.ANY),
        ],
        out_specs=(
            pl.BlockSpec(memory_space=pl.ANY),
            pl.BlockSpec(memory_space=pl.ANY),
            pl.BlockSpec(memory_space=pltpu.VMEM),
        ),
        scratch_shapes=[
            pltpu.VMEM((COLORS, 2, sites, nvec), kind),
            pltpu.VMEM((sites, 128), jnp.float32),
            pltpu.VMEM((sites, 128), jnp.float32),
            pltpu.VMEM((2 * sites, 2 * nvec), kind),
            pltpu.VMEM((nvec, 2 * nvec), jnp.float32),
            pltpu.VMEM((2, n, nrows, 2 * nvec), kind),
            pltpu.VMEM((2, n - 1, nrows, 2 * nvec), kind),
            pltpu.VMEM((nrows, 2 * nvec), kind),
            pltpu.SemaphoreType.DMA((COLORS,)),
            pltpu.SemaphoreType.DMA,
            pltpu.SemaphoreType.DMA((2, n - 1)),
            pltpu.SemaphoreType.DMA((2, n - 1)),
            pltpu.SemaphoreType.DMA((2, n - 1)),
            pltpu.SemaphoreType.DMA((2, n - 1)),
            pltpu.SemaphoreType.DMA((n,)),
            pltpu.SemaphoreType.DMA((n,)),
        ],
        compiler_params=pltpu.CompilerParams(
            collective_id=0, has_side_effects=True, vmem_limit_bytes=44 * 1024 * 1024
        ),
        cost_estimate=pl.CostEstimate(
            flops=16 * COLORS * sites * nvec * nvec,
            bytes_accessed=4 * COLORS * sites * nvec,
            transcendentals=0,
        ),
    )(momenta, vectors, tau)


def complex_left(block_re, block_im, n):
    rows = block_re.shape[0]
    cols = block_re.shape[1]
    block_re = block_re.reshape(rows, n, cols // n)
    block_im = block_im.reshape(rows, n, cols // n)
    stacked = jnp.stack(
        [jnp.stack([block_re, -block_im], axis=2), jnp.stack([block_im, block_re], axis=2)], axis=1
    )
    return stacked.reshape(2 * rows, 2 * cols)


def local(eigvec, momenta, peram):
    vectors = eigvec[0]
    nvec = vectors.shape[3]
    nrows = peram.shape[2]
    tau = peram[0].reshape(2, nrows, SPIN * nvec)
    piece, source, block = fused(vectors, momenta, tau)
    n = piece.shape[0]
    source = source.reshape(nvec, 2 * nvec)
    flat = piece.reshape(2 * nvec, SPIN * nvec)
    mixed = jnp.dot(
        complex_left(block[:, :nvec], block[:, nvec:], n), flat, preferred_element_type=jnp.float32
    ).reshape(nrows, 2, SPIN * nvec)
    mixed = mixed.astype(jnp.bfloat16)
    mixed_re = mixed[:, 0].reshape(nrows * SPIN, nvec)
    mixed_im = mixed[:, 1].reshape(nrows * SPIN, nvec)
    source_re = source[:, :nvec]
    source_im = source[:, nvec:]
    right = jnp.concatenate([source, jnp.concatenate([-source_im, source_re], axis=1)], axis=0)
    dressed = jnp.dot(
        jnp.concatenate([mixed_re, mixed_im], axis=1), right, preferred_element_type=jnp.float32
    )
    return dressed.reshape(1, nrows, SPIN, 2, nvec).astype(jnp.bfloat16)


def solution(mesh):
    return jax.shard_map(
        local,
        mesh=mesh,
        in_specs=(P("tm", None, None, "space", None), P(), P("tm", None, "space", None, None)),
        out_specs=P("tm", "space", None, None, None),
        check_vma=False,
    )
```

```python
import functools
import math

import jax
import jax.numpy as jnp
from jax import lax
from jax.experimental import pallas as pl
from jax.experimental.pallas import tpu as pltpu
from jax.sharding import PartitionSpec as P

SPIN = 4
COLORS = 3
LAT = 32
MESH = pl.DeviceIdType.MESH


def phase_tables(momenta_ref, k, first_site, count):
    sites = first_site + lax.broadcasted_iota(jnp.int32, (count, 128), 0)
    x = sites & (LAT - 1)
    y = (sites >> 5) & (LAT - 1)
    z = sites >> 10
    winding = (momenta_ref[k, 0] * x + momenta_ref[k, 1] * y + momenta_ref[k, 2] * z) & (LAT - 1)
    quadrant = (winding + 4) >> 3
    rest = (winding - (quadrant << 3)).astype(jnp.float32) * (2.0 * math.pi / LAT)
    sq = rest * rest
    sin_r = rest * (
        1.0 + sq * (-1.0 / 6 + sq * (1.0 / 120 + sq * (-1.0 / 5040 + sq * (1.0 / 362880))))
    )
    cos_r = 1.0 + sq * (
        -0.5 + sq * (1.0 / 24 + sq * (-1.0 / 720 + sq * (1.0 / 40320 + sq * (-1.0 / 3628800))))
    )
    odd = (quadrant & 1) == 1
    cos_q = jnp.where(odd, sin_r, cos_r)
    sin_q = jnp.where(odd, cos_r, sin_r)
    cos_t = jnp.where(((quadrant + 1) & 2) == 2, -cos_q, cos_q)
    sin_t = jnp.where((quadrant & 2) == 2, -sin_q, sin_q)
    return cos_t, sin_t


def fused_kernel(
    n,
    times,
    momenta_ref,
    vec_hbm,
    tau_ref,
    piece_ref,
    source_ref,
    block_ref,
    vec_ref,
    cos_ref,
    sin_ref,
    right_ref,
    acc_ref,
    inbox_ref,
    outbox_ref,
    total_ref,
    share_ref,
    load_sem,
    own_sem,
    hop_send,
    hop_recv,
    sum_send,
    sum_recv,
    all_send,
    all_recv,
):
    me_t = lax.axis_index("tm")
    me = lax.axis_index("space")
    other_t = times - 1 - me_t
    sites = vec_ref.shape[2]
    nvec = vec_ref.shape[3]
    nrows = share_ref.shape[0]

    def load(c):
        return pltpu.make_async_copy(vec_hbm.at[:, c], vec_ref.at[c], load_sem.at[c])

    for c in range(COLORS):
        load(c).start()
    own = pltpu.make_async_copy(tau_ref, piece_ref.at[me], own_sem)
    own.start()

    barrier = pltpu.get_barrier_semaphore()
    for d in range(n):
        peer = lax.rem(me + d, n)
        if d > 0:
            pl.semaphore_signal(barrier, 1, device_id=(me_t, peer), device_id_type=MESH)
        pl.semaphore_signal(barrier, 1, device_id=(other_t, peer), device_id_type=MESH)
    pl.semaphore_wait(barrier, 2 * n - 1)

    def hop(side, h, block, target):
        return pltpu.make_async_remote_copy(
            src_ref=tau_ref if h == 0 else piece_ref.at[block],
            dst_ref=piece_ref.at[block],
            send_sem=hop_send.at[side, h],
            recv_sem=hop_recv.at[side, h],
            device_id=(me_t, target),
            device_id_type=MESH,
        )

    def hop_out(side, h):
        if side == 0:
            return (me >= h) & (me + 1 < n), me - h, me + 1
        return (me + h < n) & (me >= 1), me + h, me - 1

    def hop_in(side, h):
        if side == 0:
            return me >= h + 1, me - 1 - h, me - 1
        return me + 1 + h < n, me + 1 + h, me + 1

    def start_hop(h):
        for side in range(2):
            active, block, target = hop_out(side, h)

            @pl.when(active)
            def _():
                hop(side, h, block, target).start()

    def finish_hop(h):
        for side in range(2):
            active, block, target = hop_in(side, h)

            @pl.when(active)
            def _():
                hop(side, h, block, target).wait_recv()

    def drain_hop(h):
        for side in range(2):
            active, block, target = hop_out(side, h)

            @pl.when(active)
            def _():
                hop(side, h, block, target).wait_send()

    start_hop(0)

    def tables(k):
        cos_t, sin_t = phase_tables(momenta_ref, k, me * sites, sites)
        cos_ref[...] = cos_t
        sin_ref[...] = sin_t

    def add_color(k, c):
        for lane in range(0, nvec, 128):
            real = vec_ref[c, 0, :, lane : lane + 128].astype(jnp.float32)
            imag = vec_ref[c, 1, :, lane : lane + 128].astype(jnp.float32)
            ph_re = (cos_ref[...] * real + sin_ref[...] * imag).astype(jnp.bfloat16)
            ph_im = (cos_ref[...] * imag - sin_ref[...] * real).astype(jnp.bfloat16)
            right_ref[:sites, lane : lane + 128] = ph_re
            right_ref[:sites, nvec + lane : nvec + lane + 128] = ph_im
            right_ref[sites:, lane : lane + 128] = ph_im
            right_ref[sites:, nvec + lane : nvec + lane + 128] = -ph_re
        acc_ref[k] += lax.dot_general(
            vec_ref[c].reshape(2 * sites, nvec),
            right_ref[...],
            (((0,), (0,)), ((), ())),
            preferred_element_type=jnp.float32,
        )

    def sum_copy(k, side, j):
        return pltpu.make_async_remote_copy(
            src_ref=outbox_ref.at[k, side, j],
            dst_ref=inbox_ref.at[k, side, j],
            send_sem=sum_send.at[k, side, j],
            recv_sem=sum_recv.at[k, side, j],
            device_id=(me_t, me + 1 if side == 0 else me - 1),
            device_id_type=MESH,
        )

    def rows_of(k, j):
        return acc_ref[k, j * nrows : (j + 1) * nrows, :]

    legs = []
    for i in range(1, n):
        legs.append((0, n - i))
        legs.append((1, i - 1))

    def leg_state(side, j):
        if side == 0:
            return me < j, me == 0
        return me > j, me == n - 1

    def begin_sums(k):
        for side, j in legs:
            active, first = leg_state(side, j)

            @pl.when(active & first)
            def _():
                outbox_ref[k, side, j] = rows_of(k, j).astype(jnp.bfloat16)
                sum_copy(k, side, j).start()

    def pass_sums(k):
        for side, j in legs:
            active, first = leg_state(side, j)

            @pl.when(active & jnp.logical_not(first))
            def _():
                sum_copy(k, side, j).wait_recv()
                outbox_ref[k, side, j] = (
                    rows_of(k, j) + inbox_ref[k, side, j].astype(jnp.float32)
                ).astype(jnp.bfloat16)
                sum_copy(k, side, j).start()

    def summed(k):
        total_ref[...] = acc_ref[k, pl.ds(pl.multiple_of(me * nrows, 8), nrows), :]

        @pl.when(me > 0)
        def _():
            sum_copy(k, 0, me).wait_recv()
            total_ref[...] += inbox_ref[k, 0, me].astype(jnp.float32)

        @pl.when(me < n - 1)
        def _():
            sum_copy(k, 1, me).wait_recv()
            total_ref[...] += inbox_ref[k, 1, me].astype(jnp.float32)

        return total_ref[...].astype(jnp.bfloat16)

    def drain_sums(k):
        for side, j in legs:
            active, first = leg_state(side, j)

            @pl.when(active)
            def _():
                sum_copy(k, side, j).wait_send()

    acc_ref[...] = jnp.zeros_like(acc_ref)

    tables(1)

    def source_color(c, carry):
        load(c).wait()
        add_color(1, c)
        return carry

    lax.fori_loop(0, COLORS, source_color, 0)
    begin_sums(1)

    tables(0)

    def sink_color(c, carry):
        add_color(0, c)
        return carry

    lax.fori_loop(0, COLORS - 1, sink_color, 0)
    finish_hop(0)
    if n > 2:
        start_hop(1)
    lax.fori_loop(COLORS - 1, COLORS, sink_color, 0)
    begin_sums(0)
    pass_sums(1)

    share_ref[...] = summed(1)

    def spread(d):
        peer = lax.rem(me + d, n)
        return pltpu.make_async_remote_copy(
            src_ref=share_ref,
            dst_ref=source_ref.at[me],
            send_sem=all_send.at[d],
            recv_sem=all_recv.at[me],
            device_id=(other_t, peer),
            device_id_type=MESH,
        )

    def arrival(j):
        return pltpu.make_async_remote_copy(
            src_ref=share_ref,
            dst_ref=source_ref.at[j],
            send_sem=all_send.at[j],
            recv_sem=all_recv.at[j],
            device_id=(other_t, j),
            device_id_type=MESH,
        )

    for d in range(n):
        spread(d).start()
    pass_sums(0)
    block_ref[...] = summed(0)
    for h in range(1, n - 1):
        finish_hop(h)
        if h + 1 < n - 1:
            start_hop(h + 1)
    own.wait()
    for j in range(n):
        arrival(j).wait_recv()
    for d in range(n):
        spread(d).wait_send()
    drain_sums(1)
    drain_sums(0)
    for h in range(n - 1):
        drain_hop(h)


def fused(vectors, momenta, tau):
    n = lax.axis_size("space")
    times = lax.axis_size("tm")
    sites = vectors.shape[2]
    nvec = vectors.shape[3]
    nrows = tau.shape[1]
    width = tau.shape[2]
    kind = jnp.bfloat16
    return pl.pallas_call(
        functools.partial(fused_kernel, n, times),
        out_shape=(
            jax.ShapeDtypeStruct((n, 2, nrows, width), kind),
            jax.ShapeDtypeStruct((n, nrows, 2 * nvec), kind),
            jax.ShapeDtypeStruct((nrows, 2 * nvec), kind),
        ),
        in_specs=[
            pl.BlockSpec(memory_space=pltpu.SMEM),
            pl.BlockSpec(memory_space=pl.ANY),
            pl.BlockSpec(memory_space=pl.ANY),
        ],
        out_specs=(
            pl.BlockSpec(memory_space=pl.ANY),
            pl.BlockSpec(memory_space=pl.ANY),
            pl.BlockSpec(memory_space=pltpu.VMEM),
        ),
        scratch_shapes=[
            pltpu.VMEM((COLORS, 2, sites, nvec), kind),
            pltpu.VMEM((sites, 128), jnp.float32),
            pltpu.VMEM((sites, 128), jnp.float32),
            pltpu.VMEM((2 * sites, 2 * nvec), kind),
            pltpu.VMEM((2, nvec, 2 * nvec), jnp.float32),
            pltpu.VMEM((2, 2, n, nrows, 2 * nvec), kind),
            pltpu.VMEM((2, 2, n, nrows, 2 * nvec), kind),
            pltpu.VMEM((nrows, 2 * nvec), jnp.float32),
            pltpu.VMEM((nrows, 2 * nvec), kind),
            pltpu.SemaphoreType.DMA((COLORS,)),
            pltpu.SemaphoreType.DMA,
            pltpu.SemaphoreType.DMA((2, n - 1)),
            pltpu.SemaphoreType.DMA((2, n - 1)),
            pltpu.SemaphoreType.DMA((2, 2, n)),
            pltpu.SemaphoreType.DMA((2, 2, n)),
            pltpu.SemaphoreType.DMA((n,)),
            pltpu.SemaphoreType.DMA((n,)),
        ],
        compiler_params=pltpu.CompilerParams(
            collective_id=0, has_side_effects=True, vmem_limit_bytes=60 * 1024 * 1024
        ),
        cost_estimate=pl.CostEstimate(
            flops=16 * COLORS * sites * nvec * nvec,
            bytes_accessed=4 * COLORS * sites * nvec,
            transcendentals=0,
        ),
    )(momenta, vectors, tau)


def complex_left(block_re, block_im, n):
    rows = block_re.shape[0]
    cols = block_re.shape[1]
    block_re = block_re.reshape(rows, n, cols // n)
    block_im = block_im.reshape(rows, n, cols // n)
    stacked = jnp.stack(
        [jnp.stack([block_re, -block_im], axis=2), jnp.stack([block_im, block_re], axis=2)], axis=1
    )
    return stacked.reshape(2 * rows, 2 * cols)


def local(eigvec, momenta, peram):
    vectors = eigvec[0]
    nvec = vectors.shape[3]
    nrows = peram.shape[2]
    tau = peram[0].reshape(2, nrows, SPIN * nvec)
    piece, source, block = fused(vectors, momenta, tau)
    n = piece.shape[0]
    source = source.reshape(nvec, 2 * nvec)
    flat = piece.reshape(2 * nvec, SPIN * nvec)
    mixed = jnp.dot(
        complex_left(block[:, :nvec], block[:, nvec:], n), flat, preferred_element_type=jnp.float32
    ).reshape(nrows, 2, SPIN * nvec)
    mixed = mixed.astype(jnp.bfloat16)
    mixed_re = mixed[:, 0].reshape(nrows * SPIN, nvec)
    mixed_im = mixed[:, 1].reshape(nrows * SPIN, nvec)
    source_re = source[:, :nvec]
    source_im = source[:, nvec:]
    right = jnp.concatenate([source, jnp.concatenate([-source_im, source_re], axis=1)], axis=0)
    dressed = jnp.dot(
        jnp.concatenate([mixed_re, mixed_im], axis=1), right, preferred_element_type=jnp.float32
    )
    return dressed.reshape(1, nrows, SPIN, 2, nvec).astype(jnp.bfloat16)


def solution(mesh):
    return jax.shard_map(
        local,
        mesh=mesh,
        in_specs=(P("tm", None, None, "space", None), P(), P("tm", None, "space", None, None)),
        out_specs=P("tm", "space", None, None, None),
        check_vma=False,
    )
```

```python
import functools
import math

import jax
import jax.numpy as jnp
from jax import lax
from jax.experimental import pallas as pl
from jax.experimental.pallas import tpu as pltpu
from jax.sharding import PartitionSpec as P

SPIN = 4
COLORS = 3
LAT = 32
MESH = pl.DeviceIdType.MESH


def phase_tables(momenta_ref, k, first_site, count):
    sites = first_site + lax.broadcasted_iota(jnp.int32, (count, 128), 0)
    x = sites & (LAT - 1)
    y = (sites >> 5) & (LAT - 1)
    z = sites >> 10
    winding = (momenta_ref[k, 0] * x + momenta_ref[k, 1] * y + momenta_ref[k, 2] * z) & (LAT - 1)
    quadrant = (winding + 4) >> 3
    rest = (winding - (quadrant << 3)).astype(jnp.float32) * (2.0 * math.pi / LAT)
    sq = rest * rest
    sin_r = rest * (
        1.0 + sq * (-1.0 / 6 + sq * (1.0 / 120 + sq * (-1.0 / 5040 + sq * (1.0 / 362880))))
    )
    cos_r = 1.0 + sq * (
        -0.5 + sq * (1.0 / 24 + sq * (-1.0 / 720 + sq * (1.0 / 40320 + sq * (-1.0 / 3628800))))
    )
    odd = (quadrant & 1) == 1
    cos_q = jnp.where(odd, sin_r, cos_r)
    sin_q = jnp.where(odd, cos_r, sin_r)
    cos_t = jnp.where(((quadrant + 1) & 2) == 2, -cos_q, cos_q)
    sin_t = jnp.where((quadrant & 2) == 2, -sin_q, sin_q)
    return cos_t, sin_t


def fused_kernel(
    n,
    times,
    momenta_ref,
    vec_hbm,
    tau_ref,
    piece_ref,
    source_ref,
    block_ref,
    vec_ref,
    cos_ref,
    sin_ref,
    right_ref,
    acc_ref,
    part_ref,
    slots_ref,
    share_ref,
    load_sem,
    own_sem,
    hop_send,
    hop_recv,
    sum_send,
    sum_recv,
    all_send,
    all_recv,
):
    me_t = lax.axis_index("tm")
    me = lax.axis_index("space")
    other_t = times - 1 - me_t
    sites = vec_ref.shape[2]
    nvec = vec_ref.shape[3]
    nrows = share_ref.shape[0]

    def load(c):
        return pltpu.make_async_copy(vec_hbm.at[:, c], vec_ref.at[c], load_sem.at[c])

    for c in range(COLORS):
        load(c).start()
    own = pltpu.make_async_copy(tau_ref, piece_ref.at[me], own_sem)
    own.start()

    barrier = pltpu.get_barrier_semaphore()
    for d in range(n):
        peer = lax.rem(me + d, n)
        if d > 0:
            pl.semaphore_signal(barrier, 1, device_id=(me_t, peer), device_id_type=MESH)
        pl.semaphore_signal(barrier, 1, device_id=(other_t, peer), device_id_type=MESH)
    pl.semaphore_wait(barrier, 2 * n - 1)

    def hop(side, h, part, block, target):
        return pltpu.make_async_remote_copy(
            src_ref=tau_ref.at[part] if h == 0 else piece_ref.at[block, part],
            dst_ref=piece_ref.at[block, part],
            send_sem=hop_send.at[side, h, part],
            recv_sem=hop_recv.at[side, h, part],
            device_id=(me_t, target),
            device_id_type=MESH,
        )

    def hop_out(side, h):
        if side == 0:
            return (me >= h) & (me + 1 < n), me - h, me + 1
        return (me + h < n) & (me >= 1), me + h, me - 1

    def hop_in(side, h):
        if side == 0:
            return me >= h + 1, me - 1 - h, me - 1
        return me + 1 + h < n, me + 1 + h, me + 1

    def start_hop(h, part):
        for side in range(2):
            active, block, target = hop_out(side, h)

            @pl.when(active)
            def _():
                hop(side, h, part, block, target).start()

    def finish_hop(h):
        for part in range(2):
            for side in range(2):
                active, block, target = hop_in(side, h)

                @pl.when(active)
                def _():
                    hop(side, h, part, block, target).wait_recv()

                if h + 1 < n - 1:
                    go, onward, after = hop_out(side, h + 1)

                    @pl.when(go)
                    def _():
                        hop(side, h + 1, part, onward, after).start()

    def drain_hop(h):
        for side in range(2):
            active, block, target = hop_out(side, h)

            @pl.when(active)
            def _():
                for part in range(2):
                    hop(side, h, part, block, target).wait_send()

    for part in range(2):
        start_hop(0, part)

    def tables(k):
        cos_t, sin_t = phase_tables(momenta_ref, k, me * sites, sites)
        cos_ref[...] = cos_t
        sin_ref[...] = sin_t

    def add_color(c):
        for lane in range(0, nvec, 128):
            real = vec_ref[c, 0, :, lane : lane + 128].astype(jnp.float32)
            imag = vec_ref[c, 1, :, lane : lane + 128].astype(jnp.float32)
            ph_re = (cos_ref[...] * real + sin_ref[...] * imag).astype(jnp.bfloat16)
            ph_im = (cos_ref[...] * imag - sin_ref[...] * real).astype(jnp.bfloat16)
            right_ref[:sites, lane : lane + 128] = ph_re
            right_ref[:sites, nvec + lane : nvec + lane + 128] = ph_im
            right_ref[sites:, lane : lane + 128] = ph_im
            right_ref[sites:, nvec + lane : nvec + lane + 128] = -ph_re
        acc_ref[...] += lax.dot_general(
            vec_ref[c].reshape(2 * sites, nvec),
            right_ref[...],
            (((0,), (0,)), ((), ())),
            preferred_element_type=jnp.float32,
        )

    def sum_copy(k, d):
        peer = lax.rem(me + d, n)
        return pltpu.make_async_remote_copy(
            src_ref=part_ref.at[k, peer],
            dst_ref=slots_ref.at[k, d - 1],
            send_sem=sum_send.at[k, d - 1],
            recv_sem=sum_recv.at[k, d - 1],
            device_id=(me_t, peer),
            device_id_type=MESH,
        )

    def send_parts(k):
        for j in range(n):
            part_ref[k, j] = acc_ref[j * nrows : (j + 1) * nrows, :].astype(jnp.bfloat16)
        for d in range(1, n):
            sum_copy(k, d).start()

    def summed(k):
        total = part_ref[k, me].astype(jnp.float32)
        for d in range(1, n):
            sum_copy(k, d).wait_recv()
            total = total + slots_ref[k, d - 1].astype(jnp.float32)
        return total.astype(jnp.bfloat16)

    tables(1)
    acc_ref[...] = jnp.zeros_like(acc_ref)

    def source_color(c, carry):
        load(c).wait()
        add_color(c)
        return carry

    lax.fori_loop(0, COLORS, source_color, 0)
    send_parts(1)

    tables(0)
    acc_ref[...] = jnp.zeros_like(acc_ref)

    def sink_color(c, carry):
        add_color(c)
        return carry

    lax.fori_loop(0, COLORS - 1, sink_color, 0)
    finish_hop(0)
    lax.fori_loop(COLORS - 1, COLORS, sink_color, 0)
    send_parts(0)

    share_ref[...] = summed(1)

    def spread(d):
        peer = lax.rem(me + d, n)
        return pltpu.make_async_remote_copy(
            src_ref=share_ref,
            dst_ref=source_ref.at[me],
            send_sem=all_send.at[d],
            recv_sem=all_recv.at[me],
            device_id=(other_t, peer),
            device_id_type=MESH,
        )

    def arrival(j):
        return pltpu.make_async_remote_copy(
            src_ref=share_ref,
            dst_ref=source_ref.at[j],
            send_sem=all_send.at[j],
            recv_sem=all_recv.at[j],
            device_id=(other_t, j),
            device_id_type=MESH,
        )

    for d in range(n):
        spread(d).start()
    for h in range(1, n - 1):
        finish_hop(h)
    block_ref[...] = summed(0)
    own.wait()
    for j in range(n):
        arrival(j).wait_recv()
    for d in range(n):
        spread(d).wait_send()
        if d > 0:
            sum_copy(1, d).wait_send()
            sum_copy(0, d).wait_send()
    for h in range(n - 1):
        drain_hop(h)


def fused(vectors, momenta, tau):
    n = lax.axis_size("space")
    times = lax.axis_size("tm")
    sites = vectors.shape[2]
    nvec = vectors.shape[3]
    nrows = tau.shape[1]
    width = tau.shape[2]
    kind = jnp.bfloat16
    return pl.pallas_call(
        functools.partial(fused_kernel, n, times),
        out_shape=(
            jax.ShapeDtypeStruct((n, 2, nrows, width), kind),
            jax.ShapeDtypeStruct((n, nrows, 2 * nvec), kind),
            jax.ShapeDtypeStruct((nrows, 2 * nvec), kind),
        ),
        in_specs=[
            pl.BlockSpec(memory_space=pltpu.SMEM),
            pl.BlockSpec(memory_space=pl.ANY),
            pl.BlockSpec(memory_space=pl.ANY),
        ],
        out_specs=(
            pl.BlockSpec(memory_space=pl.ANY),
            pl.BlockSpec(memory_space=pl.ANY),
            pl.BlockSpec(memory_space=pltpu.VMEM),
        ),
        scratch_shapes=[
            pltpu.VMEM((COLORS, 2, sites, nvec), kind),
            pltpu.VMEM((sites, 128), jnp.float32),
            pltpu.VMEM((sites, 128), jnp.float32),
            pltpu.VMEM((2 * sites, 2 * nvec), kind),
            pltpu.VMEM((nvec, 2 * nvec), jnp.float32),
            pltpu.VMEM((2, n, nrows, 2 * nvec), kind),
            pltpu.VMEM((2, n - 1, nrows, 2 * nvec), kind),
            pltpu.VMEM((nrows, 2 * nvec), kind),
            pltpu.SemaphoreType.DMA((COLORS,)),
            pltpu.SemaphoreType.DMA,
            pltpu.SemaphoreType.DMA((2, n - 1, 2)),
            pltpu.SemaphoreType.DMA((2, n - 1, 2)),
            pltpu.SemaphoreType.DMA((2, n - 1)),
            pltpu.SemaphoreType.DMA((2, n - 1)),
            pltpu.SemaphoreType.DMA((n,)),
            pltpu.SemaphoreType.DMA((n,)),
        ],
        compiler_params=pltpu.CompilerParams(
            collective_id=0, has_side_effects=True, vmem_limit_bytes=44 * 1024 * 1024
        ),
        cost_estimate=pl.CostEstimate(
            flops=16 * COLORS * sites * nvec * nvec,
            bytes_accessed=4 * COLORS * sites * nvec,
            transcendentals=0,
        ),
    )(momenta, vectors, tau)


def complex_left(block_re, block_im, n):
    rows = block_re.shape[0]
    cols = block_re.shape[1]
    block_re = block_re.reshape(rows, n, cols // n)
    block_im = block_im.reshape(rows, n, cols // n)
    stacked = jnp.stack(
        [jnp.stack([block_re, -block_im], axis=2), jnp.stack([block_im, block_re], axis=2)], axis=1
    )
    return stacked.reshape(2 * rows, 2 * cols)


def local(eigvec, momenta, peram):
    vectors = eigvec[0]
    nvec = vectors.shape[3]
    nrows = peram.shape[2]
    tau = peram[0].reshape(2, nrows, SPIN * nvec)
    piece, source, block = fused(vectors, momenta, tau)
    n = piece.shape[0]
    source = source.reshape(nvec, 2 * nvec)
    flat = piece.reshape(2 * nvec, SPIN * nvec)
    mixed = jnp.dot(
        complex_left(block[:, :nvec], block[:, nvec:], n), flat, preferred_element_type=jnp.float32
    ).reshape(nrows, 2, SPIN * nvec)
    mixed = mixed.astype(jnp.bfloat16)
    mixed_re = mixed[:, 0].reshape(nrows * SPIN, nvec)
    mixed_im = mixed[:, 1].reshape(nrows * SPIN, nvec)
    source_re = source[:, :nvec]
    source_im = source[:, nvec:]
    right = jnp.concatenate([source, jnp.concatenate([-source_im, source_re], axis=1)], axis=0)
    dressed = jnp.dot(
        jnp.concatenate([mixed_re, mixed_im], axis=1), right, preferred_element_type=jnp.float32
    )
    return dressed.reshape(1, nrows, SPIN, 2, nvec).astype(jnp.bfloat16)


def solution(mesh):
    return jax.shard_map(
        local,
        mesh=mesh,
        in_specs=(P("tm", None, None, "space", None), P(), P("tm", None, "space", None, None)),
        out_specs=P("tm", "space", None, None, None),
        check_vma=False,
    )
```

```python
import functools
import math

import jax
import jax.numpy as jnp
from jax import lax
from jax.experimental import pallas as pl
from jax.experimental.pallas import tpu as pltpu
from jax.sharding import PartitionSpec as P

SPIN = 4
COLORS = 3
LAT = 32
MESH = pl.DeviceIdType.MESH


def phase_tables(momenta_ref, k, first_site, count):
    sites = first_site + lax.broadcasted_iota(jnp.int32, (count, 128), 0)
    x = sites & (LAT - 1)
    y = (sites >> 5) & (LAT - 1)
    z = sites >> 10
    winding = (momenta_ref[k, 0] * x + momenta_ref[k, 1] * y + momenta_ref[k, 2] * z) & (LAT - 1)
    quadrant = (winding + 4) >> 3
    rest = (winding - (quadrant << 3)).astype(jnp.float32) * (2.0 * math.pi / LAT)
    sq = rest * rest
    sin_r = rest * (
        1.0 + sq * (-1.0 / 6 + sq * (1.0 / 120 + sq * (-1.0 / 5040 + sq * (1.0 / 362880))))
    )
    cos_r = 1.0 + sq * (
        -0.5 + sq * (1.0 / 24 + sq * (-1.0 / 720 + sq * (1.0 / 40320 + sq * (-1.0 / 3628800))))
    )
    odd = (quadrant & 1) == 1
    cos_q = jnp.where(odd, sin_r, cos_r)
    sin_q = jnp.where(odd, cos_r, sin_r)
    cos_t = jnp.where(((quadrant + 1) & 2) == 2, -cos_q, cos_q)
    sin_t = jnp.where((quadrant & 2) == 2, -sin_q, sin_q)
    return cos_t, sin_t


def fused_kernel(
    n,
    times,
    momenta_ref,
    vec_hbm,
    tau_ref,
    piece_ref,
    source_ref,
    block_ref,
    vec_ref,
    cos_ref,
    sin_ref,
    right_ref,
    acc_ref,
    part_ref,
    slots_ref,
    share_ref,
    load_sem,
    own_sem,
    hop_send,
    hop_recv,
    sum_send,
    sum_recv,
    all_send,
    all_recv,
):
    me_t = lax.axis_index("tm")
    me = lax.axis_index("space")
    other_t = times - 1 - me_t
    sites = vec_ref.shape[2]
    nvec = vec_ref.shape[3]
    nrows = share_ref.shape[0]

    def load(c):
        return pltpu.make_async_copy(vec_hbm.at[:, c], vec_ref.at[c], load_sem.at[c])

    for c in range(COLORS):
        load(c).start()
    own = pltpu.make_async_copy(tau_ref, piece_ref.at[me], own_sem)
    own.start()

    barrier = pltpu.get_barrier_semaphore()
    for d in range(n):
        peer = lax.rem(me + d, n)
        if d > 0:
            pl.semaphore_signal(barrier, 1, device_id=(me_t, peer), device_id_type=MESH)
        pl.semaphore_signal(barrier, 1, device_id=(other_t, peer), device_id_type=MESH)
    pl.semaphore_wait(barrier, 2 * n - 1)

    def hop(side, h, part, block, target):
        return pltpu.make_async_remote_copy(
            src_ref=tau_ref.at[part] if h == 0 else piece_ref.at[block, part],
            dst_ref=piece_ref.at[block, part],
            send_sem=hop_send.at[side, h, part],
            recv_sem=hop_recv.at[side, h, part],
            device_id=(me_t, target),
            device_id_type=MESH,
        )

    def hop_out(side, h):
        if side == 0:
            return (me >= h) & (me + 1 < n), me - h, me + 1
        return (me + h < n) & (me >= 1), me + h, me - 1

    def hop_in(side, h):
        if side == 0:
            return me >= h + 1, me - 1 - h, me - 1
        return me + 1 + h < n, me + 1 + h, me + 1

    def start_hop(h, part):
        for side in range(2):
            active, block, target = hop_out(side, h)

            @pl.when(active)
            def _():
                hop(side, h, part, block, target).start()

    def finish_hop(h):
        for part in range(2):
            for side in range(2):
                active, block, target = hop_in(side, h)

                @pl.when(active)
                def _():
                    hop(side, h, part, block, target).wait_recv()

                if h + 1 < n - 1:
                    go, onward, after = hop_out(side, h + 1)

                    @pl.when(go)
                    def _():
                        hop(side, h + 1, part, onward, after).start()

    def drain_hop(h):
        for side in range(2):
            active, block, target = hop_out(side, h)

            @pl.when(active)
            def _():
                for part in range(2):
                    hop(side, h, part, block, target).wait_send()

    for part in range(2):
        start_hop(0, part)

    def tables(k):
        cos_t, sin_t = phase_tables(momenta_ref, k, me * sites, sites)
        cos_ref[...] = cos_t
        sin_ref[...] = sin_t

    def add_color(c):
        for lane in range(0, nvec, 128):
            real = vec_ref[c, 0, :, lane : lane + 128].astype(jnp.float32)
            imag = vec_ref[c, 1, :, lane : lane + 128].astype(jnp.float32)
            ph_re = (cos_ref[...] * real + sin_ref[...] * imag).astype(jnp.bfloat16)
            ph_im = (cos_ref[...] * imag - sin_ref[...] * real).astype(jnp.bfloat16)
            right_ref[:sites, lane : lane + 128] = ph_re
            right_ref[:sites, nvec + lane : nvec + lane + 128] = ph_im
            right_ref[sites:, lane : lane + 128] = ph_im
            right_ref[sites:, nvec + lane : nvec + lane + 128] = -ph_re
        acc_ref[...] += lax.dot_general(
            vec_ref[c].reshape(2 * sites, nvec),
            right_ref[...],
            (((0,), (0,)), ((), ())),
            preferred_element_type=jnp.float32,
        )

    def sum_copy(k, d):
        peer = lax.rem(me + d, n)
        return pltpu.make_async_remote_copy(
            src_ref=part_ref.at[k, peer],
            dst_ref=slots_ref.at[k, d - 1],
            send_sem=sum_send.at[k, d - 1],
            recv_sem=sum_recv.at[k, d - 1],
            device_id=(me_t, peer),
            device_id_type=MESH,
        )

    def send_parts(k):
        for j in range(n):
            part_ref[k, j] = acc_ref[j * nrows : (j + 1) * nrows, :].astype(jnp.bfloat16)
        for d in range(1, n):
            sum_copy(k, d).start()

    def summed(k):
        total = part_ref[k, me].astype(jnp.float32)
        for d in range(1, n):
            sum_copy(k, d).wait_recv()
            total = total + slots_ref[k, d - 1].astype(jnp.float32)
        return total.astype(jnp.bfloat16)

    tables(1)
    acc_ref[...] = jnp.zeros_like(acc_ref)

    def source_color(c, carry):
        load(c).wait()
        add_color(c)
        return carry

    lax.fori_loop(0, COLORS, source_color, 0)
    send_parts(1)

    tables(0)
    acc_ref[...] = jnp.zeros_like(acc_ref)

    def sink_color(c, carry):
        add_color(c)
        return carry

    lax.fori_loop(0, COLORS - 1, sink_color, 0)
    finish_hop(0)
    lax.fori_loop(COLORS - 1, COLORS, sink_color, 0)
    send_parts(0)

    share_ref[...] = summed(1)

    def spread(d):
        peer = lax.rem(me + d, n)
        return pltpu.make_async_remote_copy(
            src_ref=share_ref,
            dst_ref=source_ref.at[me],
            send_sem=all_send.at[d],
            recv_sem=all_recv.at[me],
            device_id=(other_t, peer),
            device_id_type=MESH,
        )

    def arrival(j):
        return pltpu.make_async_remote_copy(
            src_ref=share_ref,
            dst_ref=source_ref.at[j],
            send_sem=all_send.at[j],
            recv_sem=all_recv.at[j],
            device_id=(other_t, j),
            device_id_type=MESH,
        )

    for d in range(n):
        spread(d).start()
    for h in range(1, n - 2):
        finish_hop(h)
    block_ref[...] = summed(0)
    if n > 2:
        finish_hop(n - 2)
    own.wait()
    for j in range(n):
        arrival(j).wait_recv()
    for d in range(n):
        spread(d).wait_send()
        if d > 0:
            sum_copy(1, d).wait_send()
            sum_copy(0, d).wait_send()
    for h in range(n - 1):
        drain_hop(h)


def fused(vectors, momenta, tau):
    n = lax.axis_size("space")
    times = lax.axis_size("tm")
    sites = vectors.shape[2]
    nvec = vectors.shape[3]
    nrows = tau.shape[1]
    width = tau.shape[2]
    kind = jnp.bfloat16
    return pl.pallas_call(
        functools.partial(fused_kernel, n, times),
        out_shape=(
            jax.ShapeDtypeStruct((n, 2, nrows, width), kind),
            jax.ShapeDtypeStruct((n, nrows, 2 * nvec), kind),
            jax.ShapeDtypeStruct((nrows, 2 * nvec), kind),
        ),
        in_specs=[
            pl.BlockSpec(memory_space=pltpu.SMEM),
            pl.BlockSpec(memory_space=pl.ANY),
            pl.BlockSpec(memory_space=pl.ANY),
        ],
        out_specs=(
            pl.BlockSpec(memory_space=pl.ANY),
            pl.BlockSpec(memory_space=pl.ANY),
            pl.BlockSpec(memory_space=pltpu.VMEM),
        ),
        scratch_shapes=[
            pltpu.VMEM((COLORS, 2, sites, nvec), kind),
            pltpu.VMEM((sites, 128), jnp.float32),
            pltpu.VMEM((sites, 128), jnp.float32),
            pltpu.VMEM((2 * sites, 2 * nvec), kind),
            pltpu.VMEM((nvec, 2 * nvec), jnp.float32),
            pltpu.VMEM((2, n, nrows, 2 * nvec), kind),
            pltpu.VMEM((2, n - 1, nrows, 2 * nvec), kind),
            pltpu.VMEM((nrows, 2 * nvec), kind),
            pltpu.SemaphoreType.DMA((COLORS,)),
            pltpu.SemaphoreType.DMA,
            pltpu.SemaphoreType.DMA((2, n - 1, 2)),
            pltpu.SemaphoreType.DMA((2, n - 1, 2)),
            pltpu.SemaphoreType.DMA((2, n - 1)),
            pltpu.SemaphoreType.DMA((2, n - 1)),
            pltpu.SemaphoreType.DMA((n,)),
            pltpu.SemaphoreType.DMA((n,)),
        ],
        compiler_params=pltpu.CompilerParams(
            collective_id=0, has_side_effects=True, vmem_limit_bytes=44 * 1024 * 1024
        ),
        cost_estimate=pl.CostEstimate(
            flops=16 * COLORS * sites * nvec * nvec,
            bytes_accessed=4 * COLORS * sites * nvec,
            transcendentals=0,
        ),
    )(momenta, vectors, tau)


def complex_left(block_re, block_im, n):
    rows = block_re.shape[0]
    cols = block_re.shape[1]
    block_re = block_re.reshape(rows, n, cols // n)
    block_im = block_im.reshape(rows, n, cols // n)
    stacked = jnp.stack(
        [jnp.stack([block_re, -block_im], axis=2), jnp.stack([block_im, block_re], axis=2)], axis=1
    )
    return stacked.reshape(2 * rows, 2 * cols)


def local(eigvec, momenta, peram):
    vectors = eigvec[0]
    nvec = vectors.shape[3]
    nrows = peram.shape[2]
    tau = peram[0].reshape(2, nrows, SPIN * nvec)
    piece, source, block = fused(vectors, momenta, tau)
    n = piece.shape[0]
    source = source.reshape(nvec, 2 * nvec)
    flat = piece.reshape(2 * nvec, SPIN * nvec)
    mixed = jnp.dot(
        complex_left(block[:, :nvec], block[:, nvec:], n), flat, preferred_element_type=jnp.float32
    ).reshape(nrows, 2, SPIN * nvec)
    mixed = mixed.astype(jnp.bfloat16)
    mixed_re = mixed[:, 0].reshape(nrows * SPIN, nvec)
    mixed_im = mixed[:, 1].reshape(nrows * SPIN, nvec)
    source_re = source[:, :nvec]
    source_im = source[:, nvec:]
    right = jnp.concatenate([source, jnp.concatenate([-source_im, source_re], axis=1)], axis=0)
    dressed = jnp.dot(
        jnp.concatenate([mixed_re, mixed_im], axis=1), right, preferred_element_type=jnp.float32
    )
    return dressed.reshape(1, nrows, SPIN, 2, nvec).astype(jnp.bfloat16)


def solution(mesh):
    return jax.shard_map(
        local,
        mesh=mesh,
        in_specs=(P("tm", None, None, "space", None), P(), P("tm", None, "space", None, None)),
        out_specs=P("tm", "space", None, None, None),
        check_vma=False,
    )
```
